32 devices in a mesh: section: 8 (over z, y), tile: 4 (over x, core).
Axes of the slice: x: 2, y: 2, z: 4, core: 2. Of those that a mesh axis runs over, the one named last changes fastest.
Arguments:
- acts: bfloat16 [8, 2, 256, 32, 128], P('section', None, None, 'tile'), may hold values from -6 to 6
- weights: bfloat16 [8, 9, 256, 256], P('section'), may hold values from -0.0625 to 0.0625
- cotangent: bfloat16 [2, 256, 32, 128], P(None, None, 'tile'), may hold values from -6 to 6
Outputs:
- grad_acts: bfloat16 [8, 2, 256, 32, 128], P('section', None, None, 'tile')
- weight_grad: float32 [8, 9, 256, 256], P('section')
The draws below stay inside these ranges and needn't reach their ends.
All inputs are finite; a program needn't handle non-finite values.
Results may differ from the reference program's by a relative error of at most 0.017.
Values may be sent and summed in bfloat16 or wider, within the bound.
A program may use at most 64 MiB of HBM per device.

```python
import jax
import jax.numpy as jnp
from jax import lax

C = 256
MB = 2
COLS = 128
LAYERS = 8
ROWS = 32


def levels(key, extent, pieces, least, high):
    level, own = 1.0, jax.random.fold_in(key, 6)
    for position, blocks in pieces:
        draws = jnp.exp(jax.random.uniform(jax.random.fold_in(own, position), (blocks,), jnp.float32, least / len(pieces), high / len(pieces)))
        level = level * jnp.repeat(draws, extent[position] // blocks).reshape([-1 if axis == position else 1 for axis in range(len(extent))])
    return level


def normal_values(rng, extent, spread, most, shards=(), kind=jnp.bfloat16):
    array = spread * jax.random.normal(rng, extent, jnp.float32)
    if shards:
        array = array * levels(rng, extent, shards, -0.22, 0.18)
    return jnp.clip(array, -most, most).astype(kind)


def setup_inputs(seed: int = 0) -> dict:
    streams_of = jax.random.split(jax.random.key(seed), 4)
    acts = normal_values(streams_of[0], (LAYERS, MB, C, ROWS, COLS), 1.0, 6.0, ((0, 8), (3, 4)))
    weights = normal_values(streams_of[1], (LAYERS, 9, C, C), (36 * C) ** -0.5, 0.0625, ((0, 8),))
    cotangent = normal_values(streams_of[2], (MB, C, ROWS, COLS), 1.0, 6.0, ((2, 4),))
    return {"acts": acts, "weights": weights, "cotangent": cotangent}


def shift_cols(field, offset):
    if offset == 0:
        return field
    zeros = jnp.zeros_like(field[..., :1])
    if offset == 1:
        return jnp.concatenate([field[..., 1:], zeros], axis=-1)
    return jnp.concatenate([zeros, field[..., :-1]], axis=-1)

def reference(acts, weights, cotangent):
    scale = 1.0 / jnp.sqrt(jnp.float32(MB * ROWS * COLS))
    upper = cotangent
    grads = []
    kernels = []
    for layer in reversed(range(LAYERS)):
        inputs = acts[layer].astype(jnp.float32)
        sigma = jax.nn.sigmoid(inputs)
        hidden = (inputs * sigma).astype(jnp.bfloat16).astype(jnp.float32)
        slope = sigma * (1.0 + inputs * (1.0 - sigma))
        grad_up = upper.astype(jnp.float32)
        kernel = weights[layer].astype(jnp.float32)
        back = jnp.zeros_like(grad_up)
        parts = []
        for row_step in (-1, 0, 1):
            for col_step in (-1, 0, 1):
                index = (row_step + 1) * 3 + col_step + 1
                moved = shift_cols(jnp.roll(grad_up, row_step, axis=2), -col_step)
                back = back + jnp.einsum('oi,gorc->girc', kernel[index], moved, precision=lax.Precision.HIGHEST)
                seen = shift_cols(jnp.roll(hidden, -row_step, axis=2), col_step)
                parts.append(jnp.einsum('gorc,girc->oi', grad_up, seen, precision=lax.Precision.HIGHEST))
        kernels.append(jnp.stack(parts) * scale)
        upper = (grad_up + back * slope).astype(jnp.bfloat16)
        grads.append(upper)
    return (jnp.stack(grads[::-1]), jnp.stack(kernels[::-1]))
```

```python
import functools

import jax
import jax.numpy as jnp
from jax import lax
from jax.experimental import pallas as pl
from jax.experimental.pallas import tpu as pltpu
from jax.sharding import PartitionSpec as P

MESH = pl.DeviceIdType.MESH


def shifted(value, offset):
    width = value.shape[-1]
    if offset == 0:
        return value
    lane = lax.broadcasted_iota(jnp.int32, value.shape, value.ndim - 1)
    moved = pltpu.roll(value, (-offset) % width, value.ndim - 1)
    edge = width - 1 if offset == 1 else 0
    return jnp.where(lane == edge, 0.0, moved)


def chain_kernel(
    n_section, n_tile, acts, wide, cot, grads, wgrad,
    rows_in, hidden3, slope, acts_rim, cot_rim,
    rim_send, rim_recv, main_send, main_recv, edge_send, edge_recv,
):
    batches, height, chans, width = acts.shape
    pair = 2
    blocks = height // pair
    s = lax.axis_index("section")
    t = lax.axis_index("tile")
    t_low = lax.rem(t + n_tile - 1, n_tile)
    t_high = lax.rem(t + 1, n_tile)
    s_low = lax.rem(s + n_section - 1, n_section)
    s_high = lax.rem(s + 1, n_section)
    top = s == n_section - 1

    barrier = pltpu.get_barrier_semaphore()
    friends = [(s, t_low), (s, t_high)]
    for other in (s_low, s_high):
        friends += [(other, t_low), (other, t), (other, t_high)]
    for friend in friends:
        pl.semaphore_signal(barrier, inc=1, device_id=friend, device_id_type=MESH)
    pl.semaphore_wait(barrier, len(friends))

    rims = []
    for which, (source, landing) in enumerate(((cot, cot_rim), (acts, acts_rim))):
        for side, (row, target) in enumerate(((height - 1, t_high), (0, t_low))):
            rims.append(
                pltpu.make_async_remote_copy(
                    src_ref=source.at[:, row],
                    dst_ref=landing.at[side],
                    send_sem=rim_send.at[which, side],
                    recv_sem=rim_recv.at[which, side],
                    device_id=(s, target),
                    device_id_type=MESH,
                )
            )
    for copy in rims:
        copy.start()

    def main_copy(m, block):
        return pltpu.make_async_remote_copy(
            src_ref=grads.at[m, pl.ds(block * pair, pair)],
            dst_ref=rows_in.at[m, pl.ds(block * pair + 1, pair)],
            send_sem=main_send.at[m, block],
            recv_sem=main_recv.at[m, block],
            device_id=(s_low, t),
            device_id_type=MESH,
        )

    def edge_copy(m, side):
        row, slot, target = ((height - 1, 0, t_high), (0, height + 1, t_low))[side]
        return pltpu.make_async_remote_copy(
            src_ref=grads.at[m, row],
            dst_ref=rows_in.at[m, slot],
            send_sem=edge_send.at[m, side],
            recv_sem=edge_recv.at[m, side],
            device_id=(s_low, target),
            device_id_type=MESH,
        )

    def fill_slope(index, carry):
        m, row = index // height, index % height
        value = acts[m, row].astype(jnp.float32)
        sigma = jax.nn.sigmoid(value)
        slope[m, row] = sigma * (1.0 + value * (1.0 - sigma))
        return carry

    lax.fori_loop(0, batches * height, fill_slope, 0)

    def put_hidden(m, slot, raw):
        value = raw.astype(jnp.float32)
        hidden = value * jax.nn.sigmoid(value)
        for place, offset in enumerate((-1, 0, 1)):
            hidden3[m, slot, pl.ds(place * chans, chans)] = shifted(hidden, offset).astype(
                jnp.bfloat16
            )

    def fill_hidden():
        def one(index, carry):
            m, row = index // height, index % height
            put_hidden(m, row + 1, acts[m, row])
            return carry

        lax.fori_loop(0, batches * height, one, 0)
        for m in range(batches):
            put_hidden(m, 0, acts_rim[0, m])
            put_hidden(m, height + 1, acts_rim[1, m])

    for copy in rims:
        copy.wait()

    @pl.when(top)
    def _():
        for m in range(batches):
            rows_in[m, 0] = cot_rim[0, m]
            rows_in[m, pl.ds(1, height)] = cot[m]
            rows_in[m, height + 1] = cot_rim[1, m]

    @pl.when(jnp.logical_not(top))
    def _():
        fill_hidden()

    wgrad[...] = jnp.zeros_like(wgrad)

    def one_batch(m, carry):
        @pl.when(jnp.logical_not(top))
        def _():
            for side in range(2):
                edge_copy(m, side).wait_recv()
            for block in range(blocks):
                main_copy(m, block).wait_recv()

        def one_block(block, inner):
            first = block * pair
            right = jnp.concatenate(
                [
                    rows_in[m, pl.ds(first + j, 3)].reshape(3 * chans, width)
                    for j in range(pair)
                ],
                axis=1,
            )
            product = jnp.dot(wide[...], right, preferred_element_type=jnp.float32)
            for j in range(pair):
                part = product[:, j * width : (j + 1) * width]
                back = part[chans : 2 * chans]
                back = back + shifted(part[:chans], 1)
                back = back + shifted(part[2 * chans :], -1)
                row = first + j
                upper = rows_in[m, row + 1].astype(jnp.float32)
                grads[m, row] = (upper + back * slope[m, row]).astype(jnp.bfloat16)

            @pl.when(s > 0)
            def _():
                main_copy(m, block).start()

                @pl.when(block == 0)
                def _():
                    edge_copy(m, 1).start()

                @pl.when(block == blocks - 1)
                def _():
                    edge_copy(m, 0).start()

            return inner

        lax.fori_loop(0, blocks, one_block, 0)

        @pl.when(jnp.logical_and(top, m == 0))
        def _():
            fill_hidden()

        left = jnp.concatenate([rows_in[m, 1 + row] for row in range(height)], axis=1)

        def one_offset(a, inner):
            seen = jnp.concatenate([hidden3[m, a + row] for row in range(height)], axis=1)
            product = lax.dot_general(
                left, seen, (((1,), (1,)), ((), ())), preferred_element_type=jnp.float32
            )
            for place in range(3):
                wgrad[3 * a + place] += product[:, place * chans : (place + 1) * chans]
            return inner

        lax.fori_loop(0, 3, one_offset, 0)
        return carry

    lax.fori_loop(0, batches, one_batch, 0)

    @pl.when(s > 0)
    def _():
        for m in range(batches):
            for side in range(2):
                edge_copy(m, side).wait_send()
            for block in range(blocks):
                main_copy(m, block).wait_send()


def per_device(acts, weights, cotangent):
    n_section = lax.axis_size("section")
    n_tile = lax.axis_size("tile")
    batches, chans, height, width = acts.shape[1:]
    rows_first = jnp.transpose(acts[0], (0, 2, 1, 3))
    cot_rows = jnp.transpose(cotangent, (0, 2, 1, 3))
    wide = weights[0].reshape(3, 3, chans, chans)[::-1]
    wide = jnp.transpose(wide, (1, 3, 0, 2)).reshape(3 * chans, 3 * chans)
    scale = 1.0 / jnp.sqrt(jnp.float32(batches * height * n_tile * width))

    vmem = pl.BlockSpec(memory_space=pltpu.VMEM)
    grads, wgrad = pl.pallas_call(
        functools.partial(chain_kernel, n_section, n_tile),
        out_shape=(
            jax.ShapeDtypeStruct((batches, height, chans, width), jnp.bfloat16),
            jax.ShapeDtypeStruct((9, chans, chans), jnp.float32),
        ),
        in_specs=[vmem] * 3,
        out_specs=(vmem, vmem),
        scratch_shapes=[
            pltpu.VMEM((batches, height + 2, chans, width), jnp.bfloat16),
            pltpu.VMEM((batches, height + 2, 3 * chans, width), jnp.bfloat16),
            pltpu.VMEM((batches, height, chans, width), jnp.float32),
            pltpu.VMEM((2, batches, chans, width), jnp.bfloat16),
            pltpu.VMEM((2, batches, chans, width), jnp.bfloat16),
            pltpu.SemaphoreType.DMA((2, 2)),
            pltpu.SemaphoreType.DMA((2, 2)),
            pltpu.SemaphoreType.DMA((batches, height // 2)),
            pltpu.SemaphoreType.DMA((batches, height // 2)),
            pltpu.SemaphoreType.DMA((batches, 2)),
            pltpu.SemaphoreType.DMA((batches, 2)),
        ],
        compiler_params=pltpu.CompilerParams(
            collective_id=0, has_side_effects=True, vmem_limit_bytes=48 * 1024 * 1024
        ),
    )(rows_first, wide, cot_rows)
    weight_grad = lax.psum(wgrad * scale, "tile")
    return (jnp.transpose(grads, (0, 2, 1, 3))[None], weight_grad[None])


def solution(mesh):
    placed = (
        P("section", None, None, "tile", None),
        P("section", None, None, None),
        P(None, None, "tile", None),
    )
    return jax.shard_map(
        per_device,
        mesh=mesh,
        in_specs=placed,
        out_specs=(P("section", None, None, "tile", None), P("section", None, None, None)),
        check_vma=False,
    )
```

```python
import functools
import math

import jax
import jax.numpy as jnp
from jax import lax
from jax.experimental import pallas as pl
from jax.experimental.pallas import tpu as pltpu
from jax.sharding import PartitionSpec as P

MESH = pl.DeviceIdType.MESH


def shifted(value, offset):
    width = value.shape[-1]
    if offset == 0:
        return value
    lane = lax.broadcasted_iota(jnp.int32, value.shape, value.ndim - 1)
    moved = pltpu.roll(value, (-offset) % width, value.ndim - 1)
    edge = width - 1 if offset == 1 else 0
    return jnp.where(lane == edge, 0.0, moved)


def chain_kernel(
    n_section, n_tile, scale, acts, wide, cot, grads, wgrad,
    rows_in, hidden3, slope, acts_rim, cot_rim,
    parts, landed, final,
    rim_send, rim_recv, main_send, main_recv, edge_send, edge_recv,
    part_send, part_recv, whole_send, whole_recv,
):
    batches, height, chans, width = acts.shape
    pair = 2
    blocks = height // pair
    s = lax.axis_index("section")
    t = lax.axis_index("tile")
    t_low = lax.rem(t + n_tile - 1, n_tile)
    t_high = lax.rem(t + 1, n_tile)
    s_low = lax.rem(s + n_section - 1, n_section)
    s_high = lax.rem(s + 1, n_section)
    top = s == n_section - 1

    barrier = pltpu.get_barrier_semaphore()
    friends = [(s, lax.rem(t + step, n_tile)) for step in range(1, n_tile)]
    for other in (s_low, s_high):
        friends += [(other, t_low), (other, t), (other, t_high)]
    for friend in friends:
        pl.semaphore_signal(barrier, inc=1, device_id=friend, device_id_type=MESH)
    pl.semaphore_wait(barrier, len(friends))

    rims = []
    for which, (source, landing) in enumerate(((cot, cot_rim), (acts, acts_rim))):
        for side, (row, target) in enumerate(((height - 1, t_high), (0, t_low))):
            rims.append(
                pltpu.make_async_remote_copy(
                    src_ref=source.at[:, row],
                    dst_ref=landing.at[side],
                    send_sem=rim_send.at[which, side],
                    recv_sem=rim_recv.at[which, side],
                    device_id=(s, target),
                    device_id_type=MESH,
                )
            )
    for copy in rims:
        copy.start()

    def main_copy(m, block):
        return pltpu.make_async_remote_copy(
            src_ref=grads.at[m, pl.ds(block * pair, pair)],
            dst_ref=rows_in.at[m, pl.ds(block * pair + 1, pair)],
            send_sem=main_send.at[m, block],
            recv_sem=main_recv.at[m, block],
            device_id=(s_low, t),
            device_id_type=MESH,
        )

    def edge_copy(m, side):
        row, slot, target = ((height - 1, 0, t_high), (0, height + 1, t_low))[side]
        return pltpu.make_async_remote_copy(
            src_ref=grads.at[m, row],
            dst_ref=rows_in.at[m, slot],
            send_sem=edge_send.at[m, side],
            recv_sem=edge_recv.at[m, side],
            device_id=(s_low, target),
            device_id_type=MESH,
        )

    def fill_slope(index, carry):
        m, row = index // height, index % height
        value = acts[m, row].astype(jnp.float32)
        sigma = jax.nn.sigmoid(value)
        slope[m, row] = sigma * (1.0 + value * (1.0 - sigma))
        return carry

    lax.fori_loop(0, batches * height, fill_slope, 0)

    def put_hidden(m, slot, raw):
        value = raw.astype(jnp.float32)
        hidden = value * jax.nn.sigmoid(value)
        for place, offset in enumerate((-1, 0, 1)):
            hidden3[m, slot, pl.ds(place * chans, chans)] = shifted(hidden, offset).astype(
                jnp.bfloat16
            )

    def fill_hidden():
        def one(index, carry):
            m, row = index // height, index % height
            put_hidden(m, row + 1, acts[m, row])
            return carry

        lax.fori_loop(0, batches * height, one, 0)
        for m in range(batches):
            put_hidden(m, 0, acts_rim[0, m])
            put_hidden(m, height + 1, acts_rim[1, m])

    for copy in rims:
        copy.wait()

    @pl.when(top)
    def _():
        for m in range(batches):
            rows_in[m, 0] = cot_rim[0, m]
            rows_in[m, pl.ds(1, height)] = cot[m]
            rows_in[m, height + 1] = cot_rim[1, m]

    @pl.when(jnp.logical_not(top))
    def _():
        fill_hidden()

    wgrad[...] = jnp.zeros_like(wgrad)

    def one_batch(m, carry):
        def one_block(step, inner):
            block = (3 * step) % 5 - 2 * (step // 3)

            @pl.when(jnp.logical_and(jnp.logical_not(top), step == 0))
            def _():
                main_copy(m, 0).wait_recv()
                edge_copy(m, 0).wait_recv()
                main_copy(m, 1).wait_recv()

            @pl.when(jnp.logical_and(jnp.logical_not(top), step == 1))
            def _():
                main_copy(m, 3).wait_recv()
                edge_copy(m, 1).wait_recv()
                main_copy(m, 2).wait_recv()

            first = block * pair
            right = jnp.concatenate(
                [
                    jnp.concatenate([rows_in[m, first + j + k] for k in (2, 1, 0)], axis=0)
                    for j in range(pair)
                ],
                axis=1,
            )
            product = jnp.dot(wide[...], right, preferred_element_type=jnp.float32)
            for j in range(pair):
                part = product[:, j * width : (j + 1) * width]
                back = part[chans : 2 * chans]
                back = back + shifted(part[:chans], 1)
                back = back + shifted(part[2 * chans :], -1)
                row = first + j
                upper = rows_in[m, row + 1].astype(jnp.float32)
                grads[m, row] = (upper + back * slope[m, row]).astype(jnp.bfloat16)

            @pl.when(s > 0)
            def _():
                main_copy(m, block).start()

                @pl.when(step == 0)
                def _():
                    edge_copy(m, 1).start()

                @pl.when(step == 1)
                def _():
                    edge_copy(m, 0).start()

            return inner

        lax.fori_loop(0, blocks, one_block, 0)

        @pl.when(jnp.logical_and(top, m == 0))
        def _():
            fill_hidden()

        left = jnp.concatenate([rows_in[m, 1 + row] for row in range(height)], axis=1)

        def one_offset(a, inner):
            seen = jnp.concatenate([hidden3[m, a + row] for row in range(height)], axis=1)
            product = lax.dot_general(
                left, seen, (((1,), (1,)), ((), ())), preferred_element_type=jnp.float32
            )
            for place in range(3):
                rows = pl.ds(pl.multiple_of((3 * a + place) * chans, chans), chans)
                wgrad[rows] += product[:, place * chans : (place + 1) * chans]
            return inner

        lax.fori_loop(0, 3, one_offset, 0)
        return carry

    lax.fori_loop(0, batches, one_batch, 0)

    share = wgrad.shape[0] // n_tile

    def rows_of(tile):
        return pl.ds(pl.multiple_of(tile * share, share), share)

    def round_part(k, carry):
        rows = pl.ds(pl.multiple_of(k * chans, chans), chans)
        parts[rows] = wgrad[rows].astype(jnp.bfloat16)
        return carry

    lax.fori_loop(0, 9, round_part, 0)
    sends = []
    for step in range(1, n_tile):
        other = lax.rem(t + step, n_tile)
        sends.append(
            pltpu.make_async_remote_copy(
                src_ref=parts.at[rows_of(other)],
                dst_ref=landed.at[step - 1],
                send_sem=part_send.at[step - 1],
                recv_sem=part_recv.at[step - 1],
                device_id=(s, other),
                device_id_type=MESH,
            )
        )
    for copy in sends:
        copy.start()
    total = wgrad[rows_of(t)]
    for step, copy in enumerate(sends):
        copy.wait_recv()
        total = total + landed[step].astype(jnp.float32)
    final[rows_of(t)] = (total * scale).astype(jnp.bfloat16)
    wholes = []
    for step in range(1, n_tile):
        wholes.append(
            pltpu.make_async_remote_copy(
                src_ref=final.at[rows_of(t)],
                dst_ref=final.at[rows_of(t)],
                send_sem=whole_send.at[step - 1],
                recv_sem=whole_recv.at[step - 1],
                device_id=(s, lax.rem(t + step, n_tile)),
                device_id_type=MESH,
            )
        )
    for copy in wholes:
        copy.start()
    for copy in sends:
        copy.wait_send()
    for copy in wholes:
        copy.wait()

    def widen(k, carry):
        rows = pl.ds(pl.multiple_of(k * chans, chans), chans)
        wgrad[rows] = final[rows].astype(jnp.float32)
        return carry

    lax.fori_loop(0, 9, widen, 0)

    @pl.when(s > 0)
    def _():
        for m in range(batches):
            for side in range(2):
                edge_copy(m, side).wait_send()
            for block in range(blocks):
                main_copy(m, block).wait_send()


def per_device(acts, weights, cotangent):
    n_section = lax.axis_size("section")
    n_tile = lax.axis_size("tile")
    batches, chans, height, width = acts.shape[1:]
    rows_first = jnp.transpose(acts[0], (0, 2, 1, 3))
    cot_rows = jnp.transpose(cotangent, (0, 2, 1, 3))
    wide = weights[0].reshape(3, 3, chans, chans)
    wide = jnp.transpose(wide, (1, 3, 0, 2)).reshape(3 * chans, 3 * chans)
    scale = 1.0 / math.sqrt(batches * height * n_tile * width)
    taps = 9 * chans

    vmem = pl.BlockSpec(memory_space=pltpu.VMEM)
    grads, wgrad = pl.pallas_call(
        functools.partial(chain_kernel, n_section, n_tile, scale),
        out_shape=(
            jax.ShapeDtypeStruct((batches, height, chans, width), jnp.bfloat16),
            jax.ShapeDtypeStruct((taps, chans), jnp.float32),
        ),
        in_specs=[vmem] * 3,
        out_specs=(vmem, vmem),
        scratch_shapes=[
            pltpu.VMEM((batches, height + 2, chans, width), jnp.bfloat16),
            pltpu.VMEM((batches, height + 2, 3 * chans, width), jnp.bfloat16),
            pltpu.VMEM((batches, height, chans, width), jnp.float32),
            pltpu.VMEM((2, batches, chans, width), jnp.bfloat16),
            pltpu.VMEM((2, batches, chans, width), jnp.bfloat16),
            pltpu.VMEM((taps, chans), jnp.bfloat16),
            pltpu.VMEM((n_tile - 1, taps // n_tile, chans), jnp.bfloat16),
            pltpu.VMEM((taps, chans), jnp.bfloat16),
            pltpu.SemaphoreType.DMA((2, 2)),
            pltpu.SemaphoreType.DMA((2, 2)),
            pltpu.SemaphoreType.DMA((batches, height // 2)),
            pltpu.SemaphoreType.DMA((batches, height // 2)),
            pltpu.SemaphoreType.DMA((batches, 2)),
            pltpu.SemaphoreType.DMA((batches, 2)),
        ]
        + [pltpu.SemaphoreType.DMA((n_tile - 1,))] * 4,
        compiler_params=pltpu.CompilerParams(
            collective_id=0, has_side_effects=True, vmem_limit_bytes=48 * 1024 * 1024
        ),
    )(rows_first, wide, cot_rows)
    weight_grad = wgrad.reshape(9, chans, chans)
    return (jnp.transpose(grads, (0, 2, 1, 3))[None], weight_grad[None])


def solution(mesh):
    placed = (
        P("section", None, None, "tile", None),
        P("section", None, None, None),
        P(None, None, "tile", None),
    )
    return jax.shard_map(
        per_device,
        mesh=mesh,
        in_specs=placed,
        out_specs=(P("section", None, None, "tile", None), P("section", None, None, None)),
        check_vma=False,
    )
```
